256 devices in a mesh: seq: 32 (over z_lo, x, core), head: 8 (over z_hi, y).
Axes of the slice: x: 4, y: 4, z: 8 (z_hi: 2, z_lo: 4; z = z_hi * 4 + z_lo), core: 2. Of those that a mesh axis runs over, the one named last changes fastest.
Arguments:
- queries: bfloat16 [6144, 3072], P(('seq', 'head')), may hold values from -9 to 9
- keys: bfloat16 [6144, 3072], P(('seq', 'head')), may hold values from -9 to 9
- values: bfloat16 [6144, 3072], P(('seq', 'head')), may hold values from -6 to 6
- d_out: bfloat16 [6144, 3072], P(('seq', 'head')), may hold values from -6 to 6
- gain: float32 [16, 3072], replicated, may hold values from 0.3 to 3
- segment_lengths: int32 [8], replicated, may hold values from 672 to 864, as said below
- segment_step: int32 [8], replicated, may hold values from 0 to 15
- block_slot: int32 [32], replicated, may hold values from 0 to 31, each once
Outputs:
- d_queries: bfloat16 [6144, 3072], P(('seq', 'head'))
- d_keys: bfloat16 [6144, 3072], P(('seq', 'head'))
- d_values: bfloat16 [6144, 3072], P(('seq', 'head'))
The draws below stay inside these ranges and needn't reach their ends.
Inputs may be any that keep to these rules, and one draw needn't show every extreme that they name: `segment_lengths`: the lengths sum to 6144; the longest is exactly 864. `block_slot`: every block position appears once.
All inputs are finite; a program needn't handle non-finite values.
Results may differ from the reference program's by a relative error of at most 0.0071.
Values may be sent and summed in bfloat16 or wider, within the bound.
No kernel may reach another device: no remote copies, remote signals or barrier semaphores. Data moves between devices by JAX's collectives and lax.ppermute only.
A program may use at most 128 MiB of HBM per device.

```python
import math
import jax
import jax.numpy as jnp
from jax import lax

HEADS = 24
HD = 128
BLK = 192
SEGMENTS = 8
STEPS = 16
WIDTH = 3072
TOKENS = 6144
N_SEQ = 32


def draw_queries(key, part):
    key = jax.random.fold_in(key, 1)
    drawn = jnp.clip(jax.random.normal(key, (TOKENS, WIDTH)), -6.0, 6.0)
    return drawn.astype(jnp.bfloat16)


def draw_keys(key, part):
    key = jax.random.fold_in(key, 2)
    drawn = jnp.clip(jax.random.normal(key, (TOKENS, WIDTH)), -6.0, 6.0)
    return drawn.astype(jnp.bfloat16)


def draw_segment_lengths(key, part):
    key = jax.random.fold_in(key, 3)
    pairs = SEGMENTS // 2
    middle = TOKENS // SEGMENTS
    spread = TOKENS // (8 * SEGMENTS)
    offsets = jax.random.randint(jax.random.fold_in(key, 1), (pairs,), 0, spread + 1)
    forced = jax.random.randint(jax.random.fold_in(key, 2), (), 0, pairs)
    offsets = jnp.where(jnp.arange(pairs, dtype=jnp.int32) == forced, spread, offsets)
    signs = 2 * jax.random.randint(jax.random.fold_in(key, 3), (pairs,), 0, 2) - 1
    moved = (signs * offsets).astype(jnp.int32)
    stacked = jnp.stack([middle + moved, middle - moved], axis=1)
    return stacked.reshape(SEGMENTS).astype(jnp.int32)


def touch_ends(drawn, own_key, low, top_value):
    longest = drawn.shape.index(max(drawn.shape))
    spots = []
    for shift in (0, 1):
        where = [jax.random.randint(jax.random.fold_in(own_key, axis), (), 0, length) for axis, length in enumerate(drawn.shape)]
        where[longest] = (where[longest] + shift) % drawn.shape[longest]
        spots.append(tuple(where))
    return drawn.at[spots[0]].set(low).at[spots[1]].set(top_value)


def steps_of(key, extent, pieces, low, high):
    factor_of = 1.0
    for position, shards_of in pieces:
        draws = jax.random.uniform(jax.random.fold_in(jax.random.fold_in(key, 6), position), (shards_of,), jnp.float32, low / len(pieces), high / len(pieces))
        factor_of = factor_of * jnp.repeat(jnp.exp(draws), extent[position] // shards_of).reshape((-1,) + (1,) * (len(extent) - 1 - position))
    return factor_of


def noise(stream_key, extent, deviation, bound, shards=(), kind=jnp.bfloat16):
    drawn = jax.random.normal(stream_key, extent, jnp.float32) * deviation
    if len(shards) > 0:
        drawn = steps_of(stream_key, extent, shards, -0.22, 0.18) * drawn
    return jnp.clip(drawn, min=-bound, max=bound).astype(kind)


def setup_inputs(seed: int = 0) -> dict:
    arg_keys = jax.random.split(jax.random.key(seed), 9)
    queries = draw_queries(jax.random.fold_in(arg_keys[8], 71), 0)
    keys = draw_keys(jax.random.fold_in(arg_keys[8], 71), 0)
    values = noise(arg_keys[2], (TOKENS, WIDTH), 1.0, 6.0, ((0, 256),))
    d_out = noise(arg_keys[3], (TOKENS, WIDTH), 1.0, 6.0, ((0, 256),))
    gain = jnp.clip(jnp.exp(jax.random.uniform(arg_keys[4], (STEPS, WIDTH), jnp.float32, math.log(0.3), math.log(3.0))), 0.3, 3.0)
    segment_lengths = draw_segment_lengths(jax.random.fold_in(arg_keys[8], 71), 0)
    segment_step = touch_ends(jax.random.randint(arg_keys[6], (SEGMENTS,), 0, STEPS), jax.random.fold_in(arg_keys[6], 1), 0, STEPS - 1).astype(jnp.int32)
    block_slot = jax.random.permutation(arg_keys[7], N_SEQ).astype(jnp.int32)
    return {"queries": queries, "keys": keys, "values": values, "d_out": d_out, "gain": gain, "segment_lengths": segment_lengths, "segment_step": segment_step, "block_slot": block_slot}


NEGATIVE = -1e+30

def segments_of(block_slot, segment_lengths):
    rows = jnp.arange(TOKENS, dtype=jnp.int32)
    positions = block_slot[rows // BLK] * BLK + rows % BLK
    bounds = jnp.cumsum(segment_lengths).astype(jnp.int32)
    return lax.optimization_barrier(jnp.sum((bounds[None, :] <= positions[:, None]).astype(jnp.int32), axis=1))

def reference(queries, keys, values, d_out, gain, segment_lengths, segment_step, block_slot):
    segs = segments_of(block_slot, segment_lengths)
    row_gain = gain[segment_step[segs]]
    d_attn = (d_out.astype(jnp.float32) * row_gain).astype(jnp.bfloat16)
    visible = segs[None, :] <= segs[:, None]
    scaling = 1.0 / math.sqrt(HD)

    def one_head(head):
        start = (head * HD).astype(jnp.int32)
        head_q = lax.dynamic_slice_in_dim(queries, start, HD, 1)
        head_k = lax.dynamic_slice_in_dim(keys, start, HD, 1)
        head_v = lax.dynamic_slice_in_dim(values, start, HD, 1)
        head_d = lax.dynamic_slice_in_dim(d_attn, start, HD, 1)
        scores = jnp.dot(head_q, head_k.T, preferred_element_type=jnp.float32) * scaling
        scores = jnp.where(visible, scores, NEGATIVE)
        row_max = lax.optimization_barrier(jnp.max(scores, axis=1))
        total = lax.optimization_barrier(jnp.sum(jnp.where(visible, jnp.exp(scores - row_max[:, None]), 0.0), axis=1))
        log_total = row_max + jnp.log(total)
        probs = jnp.where(visible, jnp.exp(scores - log_total[:, None]), 0.0)
        probs_low = probs.astype(jnp.bfloat16)
        d_probs = jnp.dot(head_d, head_v.T, preferred_element_type=jnp.float32)
        delta = lax.optimization_barrier(jnp.sum(probs * d_probs, axis=1))
        shifted = (probs * (d_probs - delta[:, None])).astype(jnp.bfloat16)
        d_query = scaling * jnp.dot(shifted, head_k, preferred_element_type=jnp.float32)
        d_key = scaling * jnp.dot(shifted.T, head_q, preferred_element_type=jnp.float32)
        d_value = jnp.dot(probs_low.T, head_d, preferred_element_type=jnp.float32)
        return (d_query, d_key, d_value)
    grads = lax.map(one_head, jnp.arange(HEADS, dtype=jnp.int32))

    def joined(stack):
        return jnp.transpose(stack, (1, 0, 2)).reshape(TOKENS, HEADS * HD).astype(jnp.bfloat16)
    return (joined(grads[0]), joined(grads[1]), joined(grads[2]))
```

```python
import functools
import math

import jax
import jax.numpy as jnp
from jax import lax
from jax.experimental import pallas as pl
from jax.experimental.pallas import tpu as pltpu
from jax.sharding import Mesh
from jax.sharding import PartitionSpec as P

HD = 128
BLK = 192
TOKENS = 6144
SEGMENTS = 8
HEADS = 24
QROWS = 768
QG = 256
GROUPS = QROWS // QG
TK = 256
X = 4
ZLO = 4
CORES = 2
NEGATIVE = -1e30
SCALING = 1.0 / math.sqrt(HD)
EXP2_SCALE = SCALING * math.log2(math.e)
COLUMNS = ("zlo", "zhi", "y")
TOKEN_AXES = ("zlo", "x", "core", "zhi", "y")


def attend_kernel(
    place, slots, lengths, steps, q_hbm, d_hbm, gain_hbm, *refs
):
    chunks = refs[0:8]
    dq_hbm = refs[8]
    dkv_mine = refs[9:13]
    dkv_other = refs[13]
    (kv, kt, q_rows, d_rows, q_cols, d_cols, gain, q_ends, scores, d_probs, dkv, dkv_low, dq_cols, dq_rows, sems) = refs[14:]
    my_x, my_core, my_head = place[0], place[1], place[2]

    def slot_at(zlo, x, core):
        return slots[zlo * (X * CORES) + x * CORES + core]

    mine = [slot_at(b, my_x, my_core) for b in range(ZLO)]
    ranks = []
    for b in range(ZLO):
        rank = jnp.int32(0)
        for other in range(ZLO):
            if other != b:
                rank = rank + (mine[other] < mine[b]).astype(jnp.int32)
        ranks.append(rank)
    ordered = []
    for r in range(ZLO):
        value = jnp.int32(0)
        for b in range(ZLO):
            value = jnp.where(ranks[b] == r, mine[b], value)
        ordered.append(value)

    copies = []
    gain_copy = pltpu.make_async_copy(
        gain_hbm.at[:, pl.ds(pl.multiple_of(my_head * HD, HD), HD)], gain, sems.at[0]
    )
    gain_copy.start()
    for b in range(ZLO):
        row = pl.ds(pl.multiple_of(ranks[b] * BLK, BLK), BLK)
        copies.append(pltpu.make_async_copy(q_hbm.at[pl.ds(b * BLK, BLK)], q_rows.at[row], sems.at[1 + b]))
        copies.append(pltpu.make_async_copy(d_hbm.at[pl.ds(b * BLK, BLK)], d_rows.at[row], sems.at[5 + b]))
    kv_copies = []
    for c in range(CORES):
        for s in range(X):
            for b in range(ZLO):
                slot = slot_at(b, (my_x + X - s) % X, (my_core + c) % CORES)
                kv_copies.append(
                    pltpu.make_async_copy(
                        chunks[c * X + s].at[pl.ds(b * BLK, BLK)],
                        kv.at[pl.ds(pl.multiple_of(slot * BLK, BLK), BLK)],
                        sems.at[9 + (c * X + s) * ZLO + b],
                    )
                )
    for copy in copies + kv_copies:
        copy.start()

    starts, ends = [], []
    total = jnp.int32(0)
    for s in range(SEGMENTS):
        starts.append(total)
        total = total + lengths[s]
        ends.append(total)

    def end_of(position):
        return sum(jnp.where(starts[s] <= position, lengths[s], 0) for s in range(SEGMENTS))

    def positions(shape, dimension):
        index = lax.broadcasted_iota(jnp.int32, shape, dimension)
        base = jnp.where(index < BLK, ordered[0] * BLK, ordered[1] * BLK - BLK)
        base = jnp.where(index < 2 * BLK, base, ordered[2] * BLK - 2 * BLK)
        base = jnp.where(index < 3 * BLK, base, ordered[3] * BLK - 3 * BLK)
        return base + index

    q_ends[...] = end_of(positions((1, QROWS), 1))
    dkv[...] = jnp.zeros_like(dkv)

    gain_copy.wait()
    for copy in copies:
        copy.wait()
    q_cols[...] = q_rows[...].T
    row_positions = positions((QROWS, HD), 0)
    row_gain = jnp.zeros((QROWS, HD), jnp.float32)
    for s in range(SEGMENTS):
        inside = (starts[s] <= row_positions) & (row_positions < ends[s])
        row_gain = jnp.where(inside, gain[pl.ds(steps[s], 1), :], row_gain)
    d_rows[...] = (d_rows[...].astype(jnp.float32) * row_gain).astype(jnp.bfloat16)
    d_cols[...] = d_rows[...].T
    for copy in kv_copies:
        copy.wait()
    for t in range(TOKENS // TK):
        kt[:, pl.ds(t * TK, TK)] = kv[pl.ds(t * TK, TK), 0:HD].T

    for g in range(GROUPS):
        lanes = slice(g * QG, (g + 1) * QG)
        first = ordered[g * QG // BLK] * BLK + g * QG % BLK
        last = ordered[((g + 1) * QG - 1) // BLK] * BLK + ((g + 1) * QG - 1) % BLK
        whole_tiles = end_of(first) // TK
        tiles = (end_of(last) + TK - 1) // TK
        qt = q_cols[:, lanes]
        dt = d_cols[:, lanes]
        limit = q_ends[:, lanes]

        def score_tile(t, top, masked):
            at = pl.ds(pl.multiple_of(t * TK, TK), TK)
            s = jnp.dot(kv[at, 0:HD], qt, preferred_element_type=jnp.float32)
            if masked:
                key_position = t * TK + lax.broadcasted_iota(jnp.int32, (TK, QG), 0)
                s = jnp.where(key_position < limit, s, NEGATIVE)
            scores[at, :] = s
            return jnp.maximum(top, jnp.max(s.reshape(TK // 8, 8, QG), axis=0))

        top = jnp.full((8, QG), NEGATIVE, jnp.float32)
        top = lax.fori_loop(0, whole_tiles, functools.partial(score_tile, masked=False), top)
        top = lax.fori_loop(whole_tiles, tiles, functools.partial(score_tile, masked=True), top)
        top = jnp.max(top, axis=0, keepdims=True)

        def weight_tile(t, carry):
            weight_sum, product_sum = carry
            at = pl.ds(pl.multiple_of(t * TK, TK), TK)
            w = jnp.exp2((scores[at, :] - top) * EXP2_SCALE)
            dp = jnp.dot(kv[at, HD:], dt, preferred_element_type=jnp.float32)
            scores[at, :] = w
            d_probs[at, :] = dp
            weight_sum = weight_sum + jnp.sum(w.reshape(TK // 8, 8, QG), axis=0)
            product_sum = product_sum + jnp.sum((w * dp).reshape(TK // 8, 8, QG), axis=0)
            return weight_sum, product_sum

        empty = jnp.zeros((8, QG), jnp.float32)
        weight_sum, product_sum = lax.fori_loop(0, tiles, weight_tile, (empty, empty))
        inverse = 1.0 / jnp.sum(weight_sum, axis=0, keepdims=True)
        delta = jnp.sum(product_sum, axis=0, keepdims=True) * inverse
        dq_cols[...] = jnp.zeros_like(dq_cols)
        q_part = q_rows[lanes, :]
        d_part = d_rows[lanes, :]

        def grad_tile(t, carry):
            at = pl.ds(pl.multiple_of(t * TK, TK), TK)
            p = scores[at, :] * inverse
            shifted = (p * (d_probs[at, :] - delta)).astype(jnp.bfloat16)
            dkv[at, HD:] += jnp.dot(p.astype(jnp.bfloat16), d_part, preferred_element_type=jnp.float32)
            dkv[at, 0:HD] += jnp.dot(shifted, q_part, preferred_element_type=jnp.float32)
            dq_cols[...] += jnp.dot(kt[:, at], shifted, preferred_element_type=jnp.float32)
            return carry

        lax.fori_loop(0, tiles, grad_tile, 0)
        dq_rows[lanes, :] = (dq_cols[...].T * SCALING).astype(jnp.bfloat16)

    dkv_low[:, 0:HD] = (dkv[:, 0:HD] * SCALING).astype(jnp.bfloat16)
    dkv_low[:, HD:] = dkv[:, HD:].astype(jnp.bfloat16)
    out_copies = []
    for b in range(ZLO):
        row = pl.ds(pl.multiple_of(ranks[b] * BLK, BLK), BLK)
        out_copies.append(pltpu.make_async_copy(dq_rows.at[row], dq_hbm.at[pl.ds(b * BLK, BLK)], sems.at[1 + b]))
    for c in range(CORES):
        for s in range(X):
            for b in range(ZLO):
                slot = slot_at(b, (my_x + s) % X, (my_core + c) % CORES)
                target = dkv_mine[s] if c == 0 else dkv_other.at[s]
                out_copies.append(
                    pltpu.make_async_copy(
                        dkv_low.at[pl.ds(pl.multiple_of(slot * BLK, BLK), BLK)],
                        target.at[pl.ds(b * BLK, BLK)],
                        sems.at[9 + (c * X + s) * ZLO + b],
                    )
                )
    for copy in out_copies:
        copy.start()
    for copy in out_copies:
        copy.wait()


def attend(place, slots, lengths, steps, q, d, gain, chunks):
    smem = pl.BlockSpec(memory_space=pltpu.SMEM)
    hbm = pl.BlockSpec(memory_space=pl.ANY)
    low = jnp.bfloat16
    outs = (
        [jax.ShapeDtypeStruct((QROWS, HD), low)]
        + [jax.ShapeDtypeStruct((QROWS, 2 * HD), low)] * X
        + [jax.ShapeDtypeStruct((X, QROWS, 2 * HD), low)]
    )
    return pl.pallas_call(
        attend_kernel,
        out_shape=outs,
        in_specs=[smem] * 4 + [hbm] * (3 + len(chunks)),
        out_specs=[hbm] * len(outs),
        scratch_shapes=[
            pltpu.VMEM((TOKENS, 2 * HD), low),
            pltpu.VMEM((HD, TOKENS), low),
            pltpu.VMEM((QROWS, HD), low),
            pltpu.VMEM((QROWS, HD), low),
            pltpu.VMEM((HD, QROWS), low),
            pltpu.VMEM((HD, QROWS), low),
            pltpu.VMEM((16, HD), jnp.float32),
            pltpu.VMEM((1, QROWS), jnp.int32),
            pltpu.VMEM((TOKENS, QG), jnp.float32),
            pltpu.VMEM((TOKENS, QG), jnp.float32),
            pltpu.VMEM((TOKENS, 2 * HD), jnp.float32),
            pltpu.VMEM((TOKENS, 2 * HD), low),
            pltpu.VMEM((HD, QG), jnp.float32),
            pltpu.VMEM((QROWS, HD), low),
            pltpu.SemaphoreType.DMA((9 + TOKENS // BLK,)),
        ],
        compiler_params=pltpu.CompilerParams(vmem_limit_bytes=48 * 1024 * 1024),
    )(place, slots, lengths, steps, q, d, gain, *chunks)


def x_shift(array, shift):
    return lax.ppermute(array, "x", [(i, (i + shift) % X) for i in range(X)])


def other_core(array):
    return lax.ppermute(array, "core", [(0, 1), (1, 0)])


def by_head(*arrays):
    rows = arrays[0].shape[0]
    parts = [a.reshape(rows, HEADS, HD).transpose(1, 0, 2) for a in arrays]
    joined = jnp.concatenate(parts, axis=2)
    return jnp.pad(joined, ((0, 32 - HEADS), (0, 0), (0, 0)))


def exchange(array):
    return lax.all_to_all(array, COLUMNS, split_axis=0, concat_axis=0, tiled=True)


def by_token(array, rows):
    return array[:HEADS].transpose(1, 0, 2).reshape(rows, HEADS * HD)


def shards(queries, keys, values, d_out, gain, lengths, steps, slots):
    rows = queries.shape[0]
    column = lax.axis_index("zlo") * 8 + lax.axis_index("zhi") * 4 + lax.axis_index("y")
    head = jnp.minimum(column, HEADS - 1)
    place = jnp.stack([lax.axis_index("x"), lax.axis_index("core"), head]).astype(jnp.int32)
    kv = exchange(by_head(keys, values)).reshape(QROWS, 2 * HD)
    q = exchange(by_head(queries)).reshape(QROWS, HD)
    d = exchange(by_head(d_out)).reshape(QROWS, HD)
    own = [kv] + [x_shift(kv, s) for s in range(1, X)]
    chunks = own + [other_core(c) for c in own]
    outs = attend(place, slots, lengths, steps, q, d, gain, chunks)
    dq, mine, other = outs[0], outs[1:5], outs[5]
    received = other_core(other)
    pair = [
        (mine[s].astype(jnp.float32) + received[s].astype(jnp.float32)).astype(jnp.bfloat16)
        for s in range(X)
    ]
    total = pair[0].astype(jnp.float32)
    for s in range(1, X):
        total = total + x_shift(pair[s], s).astype(jnp.float32)
    dq = exchange(dq.reshape(32, rows, HD))
    dkv = exchange(total.astype(jnp.bfloat16).reshape(32, rows, 2 * HD))
    return by_token(dq, rows), by_token(dkv[..., :HD], rows), by_token(dkv[..., HD:], rows)


def solution(mesh):
    split = Mesh(mesh.devices.reshape(ZLO, X, CORES, 2, 4), TOKEN_AXES)
    tokens = P(TOKEN_AXES, None)
    return jax.shard_map(
        shards,
        mesh=split,
        in_specs=(tokens,) * 4 + (P(),) * 4,
        out_specs=(tokens,) * 3,
        check_vma=False,
    )
```

```python
import functools
import math

import jax
import jax.numpy as jnp
from jax import lax
from jax.experimental import pallas as pl
from jax.experimental.pallas import tpu as pltpu
from jax.sharding import Mesh
from jax.sharding import PartitionSpec as P

HD = 128
BLK = 192
TOKENS = 6144
SEGMENTS = 8
HEADS = 24
QROWS = 768
QG = 384
GROUPS = QROWS // QG
TK = 768
PARTS = 2
TP = TK // PARTS
X = 4
ZLO = 4
CORES = 2
NEGATIVE = -1e30
SCALING = 1.0 / math.sqrt(HD)
EXP2_SCALE = SCALING * math.log2(math.e)
COLUMNS = ("zlo", "zhi", "y")
TOKEN_AXES = ("zlo", "x", "core", "zhi", "y")


def place():
    column = lax.axis_index("zlo") * 8 + lax.axis_index("zhi") * 4 + lax.axis_index("y")
    return lax.axis_index("x"), lax.axis_index("core"), jnp.minimum(column, HEADS - 1)


def attend_kernel(slots, sources, targets, lengths, steps, qd, gain, *refs):
    chunks = refs[0:8]
    dq_hbm, mine_hbm, other_hbm = refs[8:11]
    (kv, kt, q_rows, d_rows, q_cols, d_cols, head_gain, q_ends, weights, d_probs, dkv, dq_cols, dq_rows) = refs[11:24]
    (tops, weight_sums, product_sums, delta, q_sems, kv_sems, out_sems) = refs[24:]
    my_x, my_core, my_head = place()

    def slot_at(zlo, x, core):
        return slots[zlo * (X * CORES) + x * CORES + core]

    def block(index):
        return pl.ds(pl.multiple_of(index * BLK, BLK), BLK)

    mine = [slot_at(b, my_x, my_core) for b in range(ZLO)]
    ranks = []
    for b in range(ZLO):
        rank = jnp.int32(0)
        for other in range(ZLO):
            if other != b:
                rank = rank + (mine[other] < mine[b]).astype(jnp.int32)
        ranks.append(rank)
    ordered = []
    for r in range(ZLO):
        value = jnp.int32(0)
        for b in range(ZLO):
            value = jnp.where(ranks[b] == r, mine[b], value)
        ordered.append(value)

    for i in range(CORES * X):
        pltpu.make_async_copy(
            chunks[i], kv.at[i * QROWS : (i + 1) * QROWS], kv_sems.at[i]
        ).start()

    starts, ends = [], []
    total = jnp.int32(0)
    for s in range(SEGMENTS):
        starts.append(total)
        total = total + lengths[s]
        ends.append(total)

    def end_of(position):
        return sum(jnp.where(starts[s] <= position, lengths[s], 0) for s in range(SEGMENTS))

    def positions(shape, dimension):
        index = lax.broadcasted_iota(jnp.int32, shape, dimension)
        base = jnp.where(index < BLK, ordered[0] * BLK, ordered[1] * BLK - BLK)
        base = jnp.where(index < 2 * BLK, base, ordered[2] * BLK - 2 * BLK)
        base = jnp.where(index < 3 * BLK, base, ordered[3] * BLK - 3 * BLK)
        return base + index

    bounds = []
    for g in range(GROUPS):
        row = (g + 1) * QG - 1
        last = ordered[row // BLK] * BLK + row % BLK
        bounds.append((end_of(last) + TK - 1) // TK)
    whole_tiles = end_of(ordered[0] * BLK) // TK

    def for_tiles(body, split_whole=False):
        for g in range(GROUPS):
            begin = bounds[g - 1] if g else jnp.int32(0)
            lanes = slice(g * QG, QROWS)
            if split_whole and g == 0:
                lax.fori_loop(0, whole_tiles, functools.partial(body, lanes, False), 0)
                begin = whole_tiles
            lax.fori_loop(begin, bounds[g], functools.partial(body, lanes, True), 0)

    q_ends[...] = end_of(positions((1, QROWS), 1))
    tops[...] = jnp.full_like(tops, NEGATIVE)
    weight_sums[...] = jnp.zeros_like(weight_sums)
    product_sums[...] = jnp.zeros_like(product_sums)
    dq_cols[...] = jnp.zeros_like(dq_cols)

    for b in range(ZLO):
        q_rows[block(ranks[b]), :] = qd[b * BLK : (b + 1) * BLK, 0:HD]
        d_rows[block(ranks[b]), :] = qd[b * BLK : (b + 1) * BLK, HD:]
    head_gain[...] = gain[:, pl.ds(pl.multiple_of(my_head * HD, HD), HD)]
    q_cols[...] = q_rows[...].T
    row_positions = positions((QROWS, 1), 0)
    row_gain = jnp.zeros((QROWS, HD), jnp.float32)
    for s in range(SEGMENTS):
        inside = (starts[s] <= row_positions) & (row_positions < ends[s])
        row_gain = jnp.where(inside, head_gain[pl.ds(steps[s], 1), :], row_gain)
    d_rows[...] = (d_rows[...].astype(jnp.float32) * row_gain).astype(jnp.bfloat16)
    d_cols[...] = d_rows[...].T

    def rows_of(t):
        return pl.ds(pl.multiple_of(t * TK, TK), TK)

    def leave(t):
        for i in range(TK // BLK):
            slot = t * (TK // BLK) + i
            target = targets[slot]

            @pl.when(target < X * ZLO)
            def _():
                pltpu.make_async_copy(
                    dkv.at[block(slot)], mine_hbm.at[block(target)], out_sems.at[slot]
                ).start()

            @pl.when(target >= X * ZLO)
            def _():
                pltpu.make_async_copy(
                    dkv.at[block(slot)], other_hbm.at[block(target - X * ZLO)], out_sems.at[slot]
                ).start()

    def total(array):
        return jnp.sum(jnp.sum(array.reshape(-1, 8, array.shape[1]), axis=0), axis=0, keepdims=True)

    def score_tile(lanes, masked, t, carry):
        for part in range(PARTS):
            index = t * PARTS + part
            at = pl.ds(pl.multiple_of(index * TP, TP), TP)
            rows = [block(sources[index * (TP // BLK) + i]) for i in range(TP // BLK)]
            keys = jnp.concatenate([kv[row, 0:HD] for row in rows])
            values = jnp.concatenate([kv[row, HD:] for row in rows])
            kt[:, at] = keys.T
            s = jnp.dot(keys, q_cols[:, lanes], preferred_element_type=jnp.float32)
            dp = jnp.dot(values, d_cols[:, lanes], preferred_element_type=jnp.float32)
            if masked:
                key_position = index * TP + lax.broadcasted_iota(jnp.int32, s.shape, 0)
                s = jnp.where(key_position < q_ends[:, lanes], s, NEGATIVE)
            top = jnp.max(jnp.max(s.reshape(TP // 8, 8, s.shape[1]), axis=0), axis=0, keepdims=True)
            w = jnp.exp2((s - top) * EXP2_SCALE)
            weights[at, lanes] = w
            d_probs[at, lanes] = dp
            row = pl.ds(index, 1)
            tops[row, lanes] = top
            weight_sums[row, lanes] = total(w)
            product_sums[row, lanes] = total(w * dp)
        return carry

    def grad_tile(lanes, masked, t, carry):
        at = rows_of(t)
        probs, shifts = [], []
        for part in range(PARTS):
            index = t * PARTS + part
            here = pl.ds(pl.multiple_of(index * TP, TP), TP)
            p = weights[here, lanes] * weight_sums[pl.ds(index, 1), lanes]
            probs.append(p.astype(jnp.bfloat16))
            shifts.append((p * (d_probs[here, lanes] - delta[:, lanes])).astype(jnp.bfloat16))
        p, shifted = jnp.concatenate(probs), jnp.concatenate(shifts)
        dk = jnp.dot(shifted, q_rows[lanes, :], preferred_element_type=jnp.float32)
        dkv[at, 0:HD] = (dk * SCALING).astype(jnp.bfloat16)
        dv = jnp.dot(p, d_rows[lanes, :], preferred_element_type=jnp.float32)
        dkv[at, HD:] = dv.astype(jnp.bfloat16)
        dq_cols[:, lanes] += jnp.dot(kt[:, at], shifted, preferred_element_type=jnp.float32)
        leave(t)
        return carry

    def unseen_tile(t, carry):
        dkv[rows_of(t), :] = jnp.zeros((TK, 2 * HD), jnp.bfloat16)
        leave(t)
        return carry

    for i in range(CORES * X):
        pltpu.make_async_copy(
            chunks[i], kv.at[i * QROWS : (i + 1) * QROWS], kv_sems.at[i]
        ).wait()
    for_tiles(score_tile, split_whole=True)
    lax.fori_loop(bounds[GROUPS - 1], TOKENS // TK, unseen_tile, 0)
    share = jnp.exp2((tops[...] - jnp.max(tops[...], axis=0, keepdims=True)) * EXP2_SCALE)
    inverse = 1.0 / jnp.sum(weight_sums[...] * share, axis=0, keepdims=True)
    delta[...] = jnp.sum(product_sums[...] * share, axis=0, keepdims=True) * inverse
    weight_sums[...] = share * inverse
    for_tiles(grad_tile)

    dq_rows[...] = (dq_cols[...].T * SCALING).astype(jnp.bfloat16)
    out_copies = [
        pltpu.make_async_copy(dq_rows.at[block(ranks[b])], dq_hbm.at[block(b)], q_sems.at[b])
        for b in range(ZLO)
    ]
    for copy in out_copies:
        copy.start()
    for slot in range(TOKENS // BLK):
        pltpu.make_async_copy(dkv.at[block(slot)], mine_hbm.at[block(0)], out_sems.at[slot]).wait()
    for copy in out_copies:
        copy.wait()


def attend(slots, sources, targets, lengths, steps, qd, gain, chunks):
    smem = pl.BlockSpec(memory_space=pltpu.SMEM)
    hbm = pl.BlockSpec(memory_space=pl.ANY)
    low = jnp.bfloat16
    outs = [
        jax.ShapeDtypeStruct((QROWS, HD), low),
        jax.ShapeDtypeStruct((X * QROWS, 2 * HD), low),
        jax.ShapeDtypeStruct((X * QROWS, 2 * HD), low),
    ]
    return pl.pallas_call(
        attend_kernel,
        out_shape=outs,
        in_specs=[smem] * 5 + [pl.BlockSpec(memory_space=pltpu.VMEM)] * 2 + [hbm] * len(chunks),
        out_specs=[hbm] * len(outs),
        scratch_shapes=[
            pltpu.VMEM((TOKENS, 2 * HD), low),
            pltpu.VMEM((HD, TOKENS), low),
            pltpu.VMEM((QROWS, HD), low),
            pltpu.VMEM((QROWS, HD), low),
            pltpu.VMEM((HD, QROWS), low),
            pltpu.VMEM((HD, QROWS), low),
            pltpu.VMEM((16, HD), jnp.float32),
            pltpu.VMEM((1, QROWS), jnp.int32),
            pltpu.VMEM((TOKENS, QROWS), jnp.float32),
            pltpu.VMEM((TOKENS, QROWS), jnp.float32),
            pltpu.VMEM((TOKENS, 2 * HD), low),
            pltpu.VMEM((HD, QROWS), jnp.float32),
            pltpu.VMEM((QROWS, HD), low),
            pltpu.VMEM((TOKENS // TP, QROWS), jnp.float32),
            pltpu.VMEM((TOKENS // TP, QROWS), jnp.float32),
            pltpu.VMEM((TOKENS // TP, QROWS), jnp.float32),
            pltpu.VMEM((1, QROWS), jnp.float32),
            pltpu.SemaphoreType.DMA((ZLO,)),
            pltpu.SemaphoreType.DMA((CORES * X,)),
            pltpu.SemaphoreType.DMA((TOKENS // BLK,)),
        ],
        compiler_params=pltpu.CompilerParams(vmem_limit_bytes=60 * 1024 * 1024),
    )(slots, sources, targets, lengths, steps, qd, gain, *chunks)


def tables(slots):
    index = jnp.arange(ZLO * X * CORES, dtype=jnp.int32)
    holder = jnp.sum(jnp.where(slots[None, :] == index[:, None], index[None, :], 0), axis=1)
    my_x, my_core, _ = place()
    zlo, x, core = holder // (X * CORES), holder // CORES % X, holder % CORES
    side = (core + my_core) % CORES * X
    return (
        (side + (my_x - x + X) % X) * ZLO + zlo,
        (side + (x - my_x + X) % X) * ZLO + zlo,
    )


def x_shift(array, shift):
    return lax.ppermute(array, "x", [(i, (i + shift) % X) for i in range(X)])


def other_core(array):
    return lax.ppermute(array, "core", [(0, 1), (1, 0)])


def part(array, shift):
    return array[shift * QROWS : (shift + 1) * QROWS]


def by_head(*arrays):
    rows = arrays[0].shape[0]
    parts = [a.reshape(rows, HEADS, HD).transpose(1, 0, 2) for a in arrays]
    joined = jnp.concatenate(parts, axis=2)
    return jnp.pad(joined, ((0, 32 - HEADS), (0, 0), (0, 0)))


def exchange(array):
    return lax.all_to_all(array, COLUMNS, split_axis=0, concat_axis=0, tiled=True)


def by_token(array, rows):
    return array[:HEADS].transpose(1, 0, 2).reshape(rows, HEADS * HD)


def shards(queries, keys, values, d_out, gain, lengths, steps, slots):
    rows = queries.shape[0]
    kv = exchange(by_head(keys, values)).reshape(QROWS, 2 * HD)
    qd = by_head(queries, d_out)
    own = [kv] + [x_shift(kv, s) for s in range(1, X)]
    beside = other_core(kv)
    qd, beside = lax.optimization_barrier((qd, beside))
    qd = exchange(qd).reshape(QROWS, 2 * HD)
    chunks = own + [beside] + [other_core(c) for c in own[1:]]
    dq, mine, other = attend(slots, *tables(slots), lengths, steps, qd, gain, chunks)
    received = other_core(other)
    pair = [
        (part(mine, s).astype(jnp.float32) + part(received, s).astype(jnp.float32)).astype(jnp.bfloat16)
        for s in range(X)
    ]
    total = pair[0].astype(jnp.float32)
    for s in range(1, X):
        total = total + x_shift(pair[s], s).astype(jnp.float32)
    dkv = total.astype(jnp.bfloat16)
    dq = exchange(dq.reshape(32, rows, HD))
    dkv = exchange(dkv.reshape(32, rows, 2 * HD))
    return by_token(dq, rows), by_token(dkv[..., :HD], rows), by_token(dkv[..., HD:], rows)


def solution(mesh):
    split = Mesh(mesh.devices.reshape(ZLO, X, CORES, 2, 4), TOKEN_AXES)
    tokens = P(TOKEN_AXES, None)
    return jax.shard_map(
        shards,
        mesh=split,
        in_specs=(tokens,) * 4 + (P(),) * 4,
        out_specs=(tokens,) * 3,
        check_vma=False,
    )
```

```python
import functools
import math

import jax
import jax.numpy as jnp
from jax import lax
from jax.experimental import pallas as pl
from jax.experimental.pallas import tpu as pltpu
from jax.sharding import Mesh
from jax.sharding import PartitionSpec as P

HD = 128
BLK = 192
TOKENS = 6144
SEGMENTS = 8
HEADS = 24
QROWS = 768
QG = 384
GROUPS = QROWS // QG
TK = 768
SCORE_UNROLL = 2
GRAD_UNROLL = 2
PARTS = 2
TP = TK // PARTS
X = 4
ZLO = 4
CORES = 2
NEGATIVE = -1e30
SENT = (1, 3, 2, 0)
SCALING = 1.0 / math.sqrt(HD)
EXP2_SCALE = SCALING * math.log2(math.e)
COLUMNS = ("zlo", "zhi", "y")
TOKEN_AXES = ("zlo", "x", "core", "zhi", "y")


def place():
    column = lax.axis_index("zlo") * 8 + lax.axis_index("zhi") * 4 + lax.axis_index("y")
    return lax.axis_index("x"), lax.axis_index("core"), jnp.minimum(column, HEADS - 1)


def attend_kernel(slots, lengths, steps, qd, gain, *refs):
    chunks = refs[0:8]
    dq_hbm, mine_hbm, near_hbm, far_hbm = refs[8:12]
    (kv, kt, q_rows, d_rows, q_cols, d_cols, head_gain, spans, weights, d_probs, dkv, dq_cols, dq_rows) = refs[12:25]
    (tops, weight_sums, product_sums, delta, sources, targets, q_sems, kv_sems, out_sems) = refs[25:]
    my_x, my_core, my_head = place()

    def slot_at(zlo, x, core):
        return slots[zlo * (X * CORES) + x * CORES + core]

    def block(index):
        return pl.ds(pl.multiple_of(index * BLK, BLK), BLK)

    mine = [slot_at(b, my_x, my_core) for b in range(ZLO)]
    ranks = []
    for b in range(ZLO):
        rank = jnp.int32(0)
        for other in range(ZLO):
            if other != b:
                rank = rank + (mine[other] < mine[b]).astype(jnp.int32)
        ranks.append(rank)
    ordered = []
    for r in range(ZLO):
        value = jnp.int32(0)
        for b in range(ZLO):
            value = jnp.where(ranks[b] == r, mine[b], value)
        ordered.append(value)

    for i in range(CORES * X):
        pltpu.make_async_copy(
            chunks[i], kv.at[i * QROWS : (i + 1) * QROWS], kv_sems.at[i]
        ).start()

    for c in range(CORES):
        for s in range(X):
            for b in range(ZLO):
                x = (my_x + s) % X
                core = (my_core + c) % CORES
                targets[slot_at(b, x, core)] = (c * X + SENT.index(s)) * ZLO + b
                sources[slot_at(b, x, core)] = (c * X + (X - s) % X) * ZLO + b

    starts, ends = [], []
    total = jnp.int32(0)
    for s in range(SEGMENTS):
        starts.append(total)
        total = total + lengths[s]
        ends.append(total)

    def end_of(position):
        return sum(jnp.where(starts[s] <= position, lengths[s], 0) for s in range(SEGMENTS))

    def positions(shape, dimension):
        index = lax.broadcasted_iota(jnp.int32, shape, dimension)
        base = jnp.where(index < BLK, ordered[0] * BLK, ordered[1] * BLK - BLK)
        base = jnp.where(index < 2 * BLK, base, ordered[2] * BLK - 2 * BLK)
        base = jnp.where(index < 3 * BLK, base, ordered[3] * BLK - 3 * BLK)
        return base + index

    bounds = []
    for g in range(GROUPS):
        row = (g + 1) * QG - 1
        last = ordered[row // BLK] * BLK + row % BLK
        bounds.append((end_of(last) + TK - 1) // TK)

    def for_tiles(body, unroll):
        for g in range(GROUPS):
            begin, end = bounds[g - 1] if g else jnp.int32(0), bounds[g]
            lanes = slice(g * QG, QROWS)
            runs = 0
            if unroll > 1:
                runs = jnp.maximum(end - begin, 0) // unroll
                lax.fori_loop(
                    0, runs, lambda i, c: body(lanes, unroll, begin + i * unroll, c), 0
                )
            lax.fori_loop(begin + runs * unroll, end, functools.partial(body, lanes, 1), 0)

    span = lax.broadcasted_iota(jnp.int32, (HD, 1), 0)
    q_end = end_of(positions((1, QROWS), 1))
    hidden = jnp.zeros((HD, QROWS), jnp.float32)
    lane = lax.broadcasted_iota(jnp.int32, (1, HD), 1)
    low, high = jnp.full((1, HD), TOKENS, jnp.int32), jnp.zeros((1, HD), jnp.int32)
    for s in range(SEGMENTS):
        hidden = jnp.where((span == s) & (starts[s] >= q_end), NEGATIVE, hidden)
        low, high = jnp.where(lane == s, starts[s], low), jnp.where(lane == s, ends[s], high)
    q_cols[HD:, :] = hidden.astype(jnp.bfloat16)

    def mark_tile(t, carry):
        key_position = t * TK + lax.broadcasted_iota(jnp.int32, (TK, HD), 0)
        inside = (low <= key_position) & (key_position < high)
        spans[rows_of(t), :] = jnp.where(inside, 1.0, 0.0).astype(jnp.bfloat16)
        return carry

    def rows_of(t, count=1):
        return pl.ds(pl.multiple_of(t * TK, TK), count * TK)

    lax.fori_loop(0, bounds[GROUPS - 1], mark_tile, 0)
    tops[...] = jnp.full_like(tops, NEGATIVE)
    weight_sums[...] = jnp.zeros_like(weight_sums)
    product_sums[...] = jnp.zeros_like(product_sums)
    dq_cols[...] = jnp.zeros_like(dq_cols)

    for b in range(ZLO):
        q_rows[block(ranks[b]), :] = qd[b * BLK : (b + 1) * BLK, 0:HD]
        d_rows[block(ranks[b]), :] = qd[b * BLK : (b + 1) * BLK, HD:]
    head_gain[...] = gain[:, pl.ds(pl.multiple_of(my_head * HD, HD), HD)]
    q_cols[0:HD, :] = q_rows[...].T
    row_positions = positions((QROWS, 1), 0)
    row_gain = jnp.zeros((QROWS, HD), jnp.float32)
    for s in range(SEGMENTS):
        inside = (starts[s] <= row_positions) & (row_positions < ends[s])
        row_gain = jnp.where(inside, head_gain[pl.ds(steps[s], 1), :], row_gain)
    d_rows[...] = (d_rows[...].astype(jnp.float32) * row_gain).astype(jnp.bfloat16)
    d_cols[...] = d_rows[...].T

    def leave(t):
        for i in range(TK // BLK):
            slot = t * (TK // BLK) + i
            target = targets[slot]

            @pl.when(target < X * ZLO)
            def _():
                pltpu.make_async_copy(
                    dkv.at[block(slot)], mine_hbm.at[block(target)], out_sems.at[slot]
                ).start()

            @pl.when((target >= X * ZLO) & (target < (X + 2) * ZLO))
            def _():
                pltpu.make_async_copy(
                    dkv.at[block(slot)], near_hbm.at[block(target - X * ZLO)], out_sems.at[slot]
                ).start()

            @pl.when(target >= (X + 2) * ZLO)
            def _():
                pltpu.make_async_copy(
                    dkv.at[block(slot)], far_hbm.at[block(target - (X + 2) * ZLO)], out_sems.at[slot]
                ).start()

    def total(array):
        return jnp.sum(jnp.sum(array.reshape(-1, 8, array.shape[1]), axis=0), axis=0, keepdims=True)

    def score_tile(lanes, count, t, carry):
        for part in range(count * PARTS):
            index = t * PARTS + part
            at = pl.ds(pl.multiple_of(index * TP, TP), TP)
            rows = [block(sources[index * (TP // BLK) + i]) for i in range(TP // BLK)]
            keys = jnp.concatenate([kv[row, 0:HD] for row in rows])
            values = jnp.concatenate([kv[row, HD:] for row in rows])
            kt[:, at] = keys.T
            marked = jnp.concatenate([keys, spans[at, :]], axis=1)
            s = jnp.dot(marked, q_cols[:, lanes], preferred_element_type=jnp.float32)
            dp = jnp.dot(values, d_cols[:, lanes], preferred_element_type=jnp.float32)
            top = jnp.max(jnp.max(s.reshape(TP // 8, 8, s.shape[1]), axis=0), axis=0, keepdims=True)
            w = jnp.exp2((s - top) * EXP2_SCALE)
            weights[at, lanes] = w
            d_probs[at, lanes] = dp
            row = pl.ds(index, 1)
            tops[row, lanes] = top
            weight_sums[row, lanes] = total(w)
            product_sums[row, lanes] = total(w * dp)
        return carry

    def grad_tile(lanes, count, t, carry):
        at = rows_of(t, count)
        probs, shifts = [], []
        for part in range(count * PARTS):
            index = t * PARTS + part
            here = pl.ds(pl.multiple_of(index * TP, TP), TP)
            p = weights[here, lanes] * weight_sums[pl.ds(index, 1), lanes]
            probs.append(p.astype(jnp.bfloat16))
            shifts.append((p * (d_probs[here, lanes] - delta[:, lanes])).astype(jnp.bfloat16))
        p, shifted = jnp.concatenate(probs), jnp.concatenate(shifts)
        dk = jnp.dot(shifted, q_rows[lanes, :], preferred_element_type=jnp.float32)
        dkv[at, 0:HD] = (dk * SCALING).astype(jnp.bfloat16)
        dv = jnp.dot(p, d_rows[lanes, :], preferred_element_type=jnp.float32)
        dkv[at, HD:] = dv.astype(jnp.bfloat16)
        dq_cols[:, lanes] += jnp.dot(kt[:, at], shifted, preferred_element_type=jnp.float32)
        for i in range(count):
            leave(t + i)
        return carry

    def unseen_tile(t, carry):
        dkv[rows_of(t), :] = jnp.zeros((TK, 2 * HD), jnp.bfloat16)
        leave(t)
        return carry

    for i in range(CORES * X):
        pltpu.make_async_copy(
            chunks[i], kv.at[i * QROWS : (i + 1) * QROWS], kv_sems.at[i]
        ).wait()
    for_tiles(score_tile, SCORE_UNROLL)
    lax.fori_loop(bounds[GROUPS - 1], TOKENS // TK, unseen_tile, 0)
    share = jnp.exp2((tops[...] - jnp.max(tops[...], axis=0, keepdims=True)) * EXP2_SCALE)
    inverse = 1.0 / jnp.sum(weight_sums[...] * share, axis=0, keepdims=True)
    delta[...] = jnp.sum(product_sums[...] * share, axis=0, keepdims=True) * inverse
    weight_sums[...] = share * inverse
    for_tiles(grad_tile, GRAD_UNROLL)

    dq_rows[...] = (dq_cols[...].T * SCALING).astype(jnp.bfloat16)
    out_copies = [
        pltpu.make_async_copy(dq_rows.at[block(ranks[b])], dq_hbm.at[block(b)], q_sems.at[b])
        for b in range(ZLO)
    ]
    for copy in out_copies:
        copy.start()
    for slot in range(TOKENS // BLK):
        pltpu.make_async_copy(dkv.at[block(slot)], mine_hbm.at[block(0)], out_sems.at[slot]).wait()
    for copy in out_copies:
        copy.wait()


def attend(slots, lengths, steps, qd, gain, chunks):
    smem = pl.BlockSpec(memory_space=pltpu.SMEM)
    hbm = pl.BlockSpec(memory_space=pl.ANY)
    low = jnp.bfloat16
    outs = [
        jax.ShapeDtypeStruct((QROWS, HD), low),
        jax.ShapeDtypeStruct((X * QROWS, 2 * HD), low),
        jax.ShapeDtypeStruct((2 * QROWS, 2 * HD), low),
        jax.ShapeDtypeStruct((2 * QROWS, 2 * HD), low),
    ]
    return pl.pallas_call(
        attend_kernel,
        out_shape=outs,
        in_specs=[smem] * 3 + [pl.BlockSpec(memory_space=pltpu.VMEM)] * 2 + [hbm] * len(chunks),
        out_specs=[hbm] * len(outs),
        scratch_shapes=[
            pltpu.VMEM((TOKENS, 2 * HD), low),
            pltpu.VMEM((HD, TOKENS), low),
            pltpu.VMEM((QROWS, HD), low),
            pltpu.VMEM((QROWS, HD), low),
            pltpu.VMEM((2 * HD, QROWS), low),
            pltpu.VMEM((HD, QROWS), low),
            pltpu.VMEM((16, HD), jnp.float32),
            pltpu.VMEM((TOKENS, HD), low),
            pltpu.VMEM((TOKENS, QROWS), jnp.float32),
            pltpu.VMEM((TOKENS, QROWS), jnp.float32),
            pltpu.VMEM((TOKENS, 2 * HD), low),
            pltpu.VMEM((HD, QROWS), jnp.float32),
            pltpu.VMEM((QROWS, HD), low),
            pltpu.VMEM((TOKENS // TP, QROWS), jnp.float32),
            pltpu.VMEM((TOKENS // TP, QROWS), jnp.float32),
            pltpu.VMEM((TOKENS // TP, QROWS), jnp.float32),
            pltpu.VMEM((1, QROWS), jnp.float32),
            pltpu.SMEM((TOKENS // BLK,), jnp.int32),
            pltpu.SMEM((TOKENS // BLK,), jnp.int32),
            pltpu.SemaphoreType.DMA((ZLO,)),
            pltpu.SemaphoreType.DMA((CORES * X,)),
            pltpu.SemaphoreType.DMA((TOKENS // BLK,)),
        ],
        compiler_params=pltpu.CompilerParams(vmem_limit_bytes=60 * 1024 * 1024),
    )(slots, lengths, steps, qd, gain, *chunks)


def x_shift(array, shift):
    return lax.ppermute(array, "x", [(i, (i + shift) % X) for i in range(X)])


def other_core(array):
    return lax.ppermute(array, "core", [(0, 1), (1, 0)])


def part(array, shift):
    at = SENT.index(shift) * QROWS % array.shape[0]
    return array[at : at + QROWS]


def by_head(*arrays):
    rows = arrays[0].shape[0]
    parts = [a.reshape(rows, HEADS, HD).transpose(1, 0, 2) for a in arrays]
    joined = jnp.concatenate(parts, axis=2)
    return jnp.pad(joined, ((0, 32 - HEADS), (0, 0), (0, 0)))


def exchange(array):
    return lax.all_to_all(array, COLUMNS, split_axis=0, concat_axis=0, tiled=True)


def by_token(array, rows):
    return array[:HEADS].transpose(1, 0, 2).reshape(rows, HEADS * HD)


def shards(queries, keys, values, d_out, gain, lengths, steps, slots):
    rows = queries.shape[0]
    kv = exchange(by_head(keys, values)).reshape(QROWS, 2 * HD)
    beside = other_core(kv)
    near = {s: x_shift(kv, s) for s in (1, 3)}
    later, queries, d_out, beside = lax.optimization_barrier((kv, queries, d_out, beside))
    own = [kv, near[1], x_shift(later, 2), near[3]]
    qd = exchange(by_head(queries, d_out)).reshape(QROWS, 2 * HD)
    chunks = own + [beside] + [other_core(c) for c in own[1:]]
    dq, mine, other_near, other_far = attend(slots, lengths, steps, qd, gain, chunks)
    received_near, received_far = other_core(other_near), other_core(other_far)

    def pair(shift, received):
        return part(mine, shift).astype(jnp.float32) + part(received, shift).astype(jnp.float32)

    pairs = [pair(s, received_near).astype(jnp.bfloat16) for s in SENT[:2]]
    arrived = [x_shift(p, s) for p, s in zip(pairs, SENT)]
    received_far, *_ = lax.optimization_barrier((received_far, *pairs))
    arrived.append(x_shift(pair(2, received_far).astype(jnp.bfloat16), 2))
    total = pair(0, received_far)
    for array in arrived:
        total = total + array.astype(jnp.float32)
    dkv = total.astype(jnp.bfloat16)
    dq = exchange(dq.reshape(32, rows, HD))
    dkv = exchange(dkv.reshape(32, rows, 2 * HD))
    return by_token(dq, rows), by_token(dkv[..., :HD], rows), by_token(dkv[..., HD:], rows)


def solution(mesh):
    split = Mesh(mesh.devices.reshape(ZLO, X, CORES, 2, 4), TOKEN_AXES)
    tokens = P(TOKEN_AXES, None)
    return jax.shard_map(
        shards,
        mesh=split,
        in_specs=(tokens,) * 4 + (P(),) * 4,
        out_specs=(tokens,) * 3,
        check_vma=False,
    )
```

```python
import functools
import math

import jax
import jax.numpy as jnp
from jax import lax
from jax.experimental import pallas as pl
from jax.experimental.pallas import tpu as pltpu
from jax.sharding import Mesh
from jax.sharding import PartitionSpec as P

HD = 128
BLK = 192
TOKENS = 6144
SEGMENTS = 8
HEADS = 24
QROWS = 768
QG = 384
GROUPS = QROWS // QG
TK = 768
SCORE_UNROLL = 2
GRAD_UNROLL = 2
PARTS = 2
TP = TK // PARTS
X = 4
ZLO = 4
CORES = 2
NEGATIVE = -1e30
SENT = (1, 3, 2, 0)
SCALING = 1.0 / math.sqrt(HD)
EXP2_SCALE = SCALING * math.log2(math.e)
COLUMNS = ("zlo", "zhi", "y")
TOKEN_AXES = ("zlo", "x", "core", "zhi", "y")


def place():
    column = lax.axis_index("zlo") * 8 + lax.axis_index("zhi") * 4 + lax.axis_index("y")
    return lax.axis_index("x"), lax.axis_index("core"), jnp.minimum(column, HEADS - 1)


def attend_kernel(slots, lengths, steps, qd, gain, *refs):
    chunks = refs[0:8]
    dq_hbm, out_hbm = refs[8], refs[9:13]
    (kv, kt, q_rows, d_rows, q_cols, d_cols, head_gain, spans, weights, d_probs, dkv, dq_cols, dq_rows) = refs[13:26]
    (tops, weight_sums, product_sums, delta, sources, targets, q_sems, kv_sems, out_sems) = refs[26:]
    my_x, my_core, my_head = place()

    def slot_at(zlo, x, core):
        return slots[zlo * (X * CORES) + x * CORES + core]

    def block(index):
        return pl.ds(pl.multiple_of(index * BLK, BLK), BLK)

    mine = [slot_at(b, my_x, my_core) for b in range(ZLO)]
    ranks = []
    for b in range(ZLO):
        rank = jnp.int32(0)
        for other in range(ZLO):
            if other != b:
                rank = rank + (mine[other] < mine[b]).astype(jnp.int32)
        ranks.append(rank)
    ordered = []
    for r in range(ZLO):
        value = jnp.int32(0)
        for b in range(ZLO):
            value = jnp.where(ranks[b] == r, mine[b], value)
        ordered.append(value)

    for i in range(CORES * X):
        pltpu.make_async_copy(
            chunks[i], kv.at[i * QROWS : (i + 1) * QROWS], kv_sems.at[i]
        ).start()

    for c in range(CORES):
        for s in range(X):
            for b in range(ZLO):
                x = (my_x + s) % X
                core = (my_core + c) % CORES
                targets[slot_at(b, x, core)] = (c * X + SENT.index(s)) * ZLO + b
                sources[slot_at(b, x, core)] = (c * X + (X - s) % X) * ZLO + b

    starts, ends = [], []
    total = jnp.int32(0)
    for s in range(SEGMENTS):
        starts.append(total)
        total = total + lengths[s]
        ends.append(total)

    def end_of(position):
        return sum(jnp.where(starts[s] <= position, lengths[s], 0) for s in range(SEGMENTS))

    def gain_at(position):
        span = sum((ends[s] <= position).astype(jnp.int32) for s in range(SEGMENTS))
        return head_gain[pl.ds(steps[span], 1), :]

    def positions(shape, dimension):
        index = lax.broadcasted_iota(jnp.int32, shape, dimension)
        base = jnp.where(index < BLK, ordered[0] * BLK, ordered[1] * BLK - BLK)
        base = jnp.where(index < 2 * BLK, base, ordered[2] * BLK - 2 * BLK)
        base = jnp.where(index < 3 * BLK, base, ordered[3] * BLK - 3 * BLK)
        return base + index

    bounds = []
    for g in range(GROUPS):
        row = (g + 1) * QG - 1
        last = ordered[row // BLK] * BLK + row % BLK
        bounds.append((end_of(last) + TK - 1) // TK)

    def for_tiles(body, unroll):
        for g in range(GROUPS):
            begin, end = bounds[g - 1] if g else jnp.int32(0), bounds[g]
            lanes = slice(g * QG, QROWS)
            runs = 0
            if unroll > 1:
                runs = jnp.maximum(end - begin, 0) // unroll
                lax.fori_loop(
                    0, runs, lambda i, c: body(lanes, unroll, begin + i * unroll, c), 0
                )
            lax.fori_loop(begin + runs * unroll, end, functools.partial(body, lanes, 1), 0)

    span = lax.broadcasted_iota(jnp.int32, (HD, 1), 0)
    q_end = end_of(positions((1, QROWS), 1))
    hidden = jnp.zeros((HD, QROWS), jnp.float32)
    lane = lax.broadcasted_iota(jnp.int32, (1, HD), 1)
    low, high = jnp.full((1, HD), TOKENS, jnp.int32), jnp.zeros((1, HD), jnp.int32)
    for s in range(SEGMENTS):
        hidden = jnp.where((span == s) & (starts[s] >= q_end), NEGATIVE, hidden)
        low, high = jnp.where(lane == s, starts[s], low), jnp.where(lane == s, ends[s], high)
    q_cols[HD:, :] = hidden.astype(jnp.bfloat16)

    def mark_tile(t, carry):
        key_position = t * TK + lax.broadcasted_iota(jnp.int32, (TK, HD), 0)
        inside = (low <= key_position) & (key_position < high)
        spans[rows_of(t), :] = jnp.where(inside, 1.0, 0.0).astype(jnp.bfloat16)
        return carry

    def rows_of(t, count=1):
        return pl.ds(pl.multiple_of(t * TK, TK), count * TK)

    lax.fori_loop(0, bounds[GROUPS - 1], mark_tile, 0)
    tops[...] = jnp.full_like(tops, NEGATIVE)
    weight_sums[...] = jnp.zeros_like(weight_sums)
    product_sums[...] = jnp.zeros_like(product_sums)
    dq_cols[...] = jnp.zeros_like(dq_cols)

    for b in range(ZLO):
        q_rows[block(ranks[b]), :] = qd[b * BLK : (b + 1) * BLK, 0:HD]
        d_rows[block(ranks[b]), :] = qd[b * BLK : (b + 1) * BLK, HD:]
    head_gain[...] = gain[:, pl.ds(pl.multiple_of(my_head * HD, HD), HD)]
    q_cols[0:HD, :] = q_rows[...].T
    for r in range(ZLO):
        at = slice(r * BLK, (r + 1) * BLK)
        first, last = ordered[r] * BLK, (ordered[r] + 1) * BLK - 1
        early = lax.broadcasted_iota(jnp.int32, (BLK, 1), 0) + first < end_of(first)
        row_gain = jnp.where(early, gain_at(first), gain_at(last))
        d_rows[at, :] = (d_rows[at, :].astype(jnp.float32) * row_gain).astype(jnp.bfloat16)
    d_cols[...] = d_rows[...].T

    def leave(t):
        for i in range(TK // BLK):
            slot = t * (TK // BLK) + i
            target = targets[slot]

            for i in range(4):

                @pl.when((target >= i * 2 * ZLO) & (target < (i + 1) * 2 * ZLO))
                def _():
                    pltpu.make_async_copy(
                        dkv.at[block(slot)], out_hbm[i].at[block(target - i * 2 * ZLO)], out_sems.at[slot]
                    ).start()

    def total(array):
        return jnp.sum(jnp.sum(array.reshape(-1, 8, array.shape[1]), axis=0), axis=0, keepdims=True)

    def score_tile(lanes, count, t, carry):
        for part in range(count * PARTS):
            index = t * PARTS + part
            at = pl.ds(pl.multiple_of(index * TP, TP), TP)
            rows = [block(sources[index * (TP // BLK) + i]) for i in range(TP // BLK)]
            keys = jnp.concatenate([kv[row, 0:HD] for row in rows])
            values = jnp.concatenate([kv[row, HD:] for row in rows])
            kt[:, at] = keys.T
            marked = jnp.concatenate([keys, spans[at, :]], axis=1)
            s = jnp.dot(marked, q_cols[:, lanes], preferred_element_type=jnp.float32)
            dp = jnp.dot(values, d_cols[:, lanes], preferred_element_type=jnp.float32)
            top = jnp.max(jnp.max(s.reshape(TP // 8, 8, s.shape[1]), axis=0), axis=0, keepdims=True)
            w = jnp.exp2((s - top) * EXP2_SCALE)
            weights[at, lanes] = w
            d_probs[at, lanes] = dp
            row = pl.ds(index, 1)
            tops[row, lanes] = top
            weight_sums[row, lanes] = total(w)
            product_sums[row, lanes] = total(w * dp)
        return carry

    def grad_tile(lanes, count, t, carry):
        at = rows_of(t, count)
        probs, shifts = [], []
        for part in range(count * PARTS):
            index = t * PARTS + part
            here = pl.ds(pl.multiple_of(index * TP, TP), TP)
            p = weights[here, lanes] * weight_sums[pl.ds(index, 1), lanes]
            probs.append(p.astype(jnp.bfloat16))
            shifts.append((p * (d_probs[here, lanes] - delta[:, lanes])).astype(jnp.bfloat16))
        p, shifted = jnp.concatenate(probs), jnp.concatenate(shifts)
        dk = jnp.dot(shifted, q_rows[lanes, :], preferred_element_type=jnp.float32)
        dkv[at, 0:HD] = (dk * SCALING).astype(jnp.bfloat16)
        dv = jnp.dot(p, d_rows[lanes, :], preferred_element_type=jnp.float32)
        dkv[at, HD:] = dv.astype(jnp.bfloat16)
        dq_cols[:, lanes] += jnp.dot(kt[:, at], shifted, preferred_element_type=jnp.float32)
        for i in range(count):
            leave(t + i)
        return carry

    def unseen_tile(t, carry):
        dkv[rows_of(t), :] = jnp.zeros((TK, 2 * HD), jnp.bfloat16)
        leave(t)
        return carry

    for i in range(CORES * X):
        pltpu.make_async_copy(
            chunks[i], kv.at[i * QROWS : (i + 1) * QROWS], kv_sems.at[i]
        ).wait()
    for_tiles(score_tile, SCORE_UNROLL)
    lax.fori_loop(bounds[GROUPS - 1], TOKENS // TK, unseen_tile, 0)
    share = jnp.exp2((tops[...] - jnp.max(tops[...], axis=0, keepdims=True)) * EXP2_SCALE)
    inverse = 1.0 / jnp.sum(weight_sums[...] * share, axis=0, keepdims=True)
    delta[...] = jnp.sum(product_sums[...] * share, axis=0, keepdims=True) * inverse
    weight_sums[...] = share * inverse
    for_tiles(grad_tile, GRAD_UNROLL)

    dq_rows[...] = (dq_cols[...].T * SCALING).astype(jnp.bfloat16)
    out_copies = [
        pltpu.make_async_copy(dq_rows.at[block(ranks[b])], dq_hbm.at[block(b)], q_sems.at[b])
        for b in range(ZLO)
    ]
    for copy in out_copies:
        copy.start()
    for slot in range(TOKENS // BLK):
        pltpu.make_async_copy(dkv.at[block(slot)], out_hbm[0].at[block(0)], out_sems.at[slot]).wait()
    for copy in out_copies:
        copy.wait()


def attend(slots, lengths, steps, qd, gain, chunks):
    smem = pl.BlockSpec(memory_space=pltpu.SMEM)
    hbm = pl.BlockSpec(memory_space=pl.ANY)
    low = jnp.bfloat16
    outs = [
        jax.ShapeDtypeStruct((QROWS, HD), low),
    ] + [jax.ShapeDtypeStruct((2 * QROWS, 2 * HD), low)] * 4
    return pl.pallas_call(
        attend_kernel,
        out_shape=outs,
        in_specs=[smem] * 3 + [pl.BlockSpec(memory_space=pltpu.VMEM)] * 2 + [hbm] * len(chunks),
        out_specs=[hbm] * len(outs),
        scratch_shapes=[
            pltpu.VMEM((TOKENS, 2 * HD), low),
            pltpu.VMEM((HD, TOKENS), low),
            pltpu.VMEM((QROWS, HD), low),
            pltpu.VMEM((QROWS, HD), low),
            pltpu.VMEM((2 * HD, QROWS), low),
            pltpu.VMEM((HD, QROWS), low),
            pltpu.VMEM((16, HD), jnp.float32),
            pltpu.VMEM((TOKENS, HD), low),
            pltpu.VMEM((TOKENS, QROWS), jnp.float32),
            pltpu.VMEM((TOKENS, QROWS), jnp.float32),
            pltpu.VMEM((TOKENS, 2 * HD), low),
            pltpu.VMEM((HD, QROWS), jnp.float32),
            pltpu.VMEM((QROWS, HD), low),
            pltpu.VMEM((TOKENS // TP, QROWS), jnp.float32),
            pltpu.VMEM((TOKENS // TP, QROWS), jnp.float32),
            pltpu.VMEM((TOKENS // TP, QROWS), jnp.float32),
            pltpu.VMEM((1, QROWS), jnp.float32),
            pltpu.SMEM((TOKENS // BLK,), jnp.int32),
            pltpu.SMEM((TOKENS // BLK,), jnp.int32),
            pltpu.SemaphoreType.DMA((ZLO,)),
            pltpu.SemaphoreType.DMA((CORES * X,)),
            pltpu.SemaphoreType.DMA((TOKENS // BLK,)),
        ],
        compiler_params=pltpu.CompilerParams(vmem_limit_bytes=60 * 1024 * 1024),
    )(slots, lengths, steps, qd, gain, *chunks)


def x_shift(array, shift):
    return lax.ppermute(array, "x", [(i, (i + shift) % X) for i in range(X)])


def other_core(array):
    return lax.ppermute(array, "core", [(0, 1), (1, 0)])


def part(array, shift):
    at = SENT.index(shift) * QROWS % array.shape[0]
    return array[at : at + QROWS]


def by_head(*arrays):
    rows = arrays[0].shape[0]
    parts = [a.reshape(rows, HEADS, HD).transpose(1, 0, 2) for a in arrays]
    joined = jnp.concatenate(parts, axis=2)
    return jnp.pad(joined, ((0, 32 - HEADS), (0, 0), (0, 0)))


def exchange(array):
    return lax.all_to_all(array, COLUMNS, split_axis=0, concat_axis=0, tiled=True)


def by_token(array, rows):
    return array[:HEADS].transpose(1, 0, 2).reshape(rows, HEADS * HD)


def shards(queries, keys, values, d_out, gain, lengths, steps, slots):
    rows = queries.shape[0]
    kv = exchange(by_head(keys, values)).reshape(QROWS, 2 * HD)
    beside = other_core(kv)
    near = {s: x_shift(kv, s) for s in (1, 3)}
    queries, d_out, beside = lax.optimization_barrier((queries, d_out, beside))
    later, qd = lax.optimization_barrier((kv, by_head(queries, d_out)))
    own = [kv, near[1], x_shift(later, 2), near[3]]
    qd = exchange(qd).reshape(QROWS, 2 * HD)
    chunks = own + [beside] + [other_core(c) for c in own[1:]]
    dq, near, far, other_near, other_far = attend(slots, lengths, steps, qd, gain, chunks)
    received_near = other_core(other_near)
    other_far, received_near = lax.optimization_barrier((other_far, received_near))
    received_far = other_core(other_far)

    def pair(shift, received):
        return part(near if shift in SENT[:2] else far, shift).astype(jnp.float32) + part(received, shift).astype(jnp.float32)

    pairs = [pair(s, received_near).astype(jnp.bfloat16) for s in SENT[:2]]
    arrived = [x_shift(p, s) for p, s in zip(pairs, SENT)]
    received_far, *_ = lax.optimization_barrier((received_far, *pairs))
    arrived.append(x_shift(pair(2, received_far).astype(jnp.bfloat16), 2))
    total = pair(0, received_far)
    for array in arrived:
        total = total + array.astype(jnp.float32)
    dkv = total.astype(jnp.bfloat16)
    dq = exchange(dq.reshape(32, rows, HD))
    dkv = exchange(dkv.reshape(32, rows, 2 * HD))
    return by_token(dq, rows), by_token(dkv[..., :HD], rows), by_token(dkv[..., HD:], rows)


def solution(mesh):
    split = Mesh(mesh.devices.reshape(ZLO, X, CORES, 2, 4), TOKEN_AXES)
    tokens = P(TOKEN_AXES, None)
    return jax.shard_map(
        shards,
        mesh=split,
        in_specs=(tokens,) * 4 + (P(),) * 4,
        out_specs=(tokens,) * 3,
        check_vma=False,
    )
```
